32 devices in a mesh: read: 8 (over z, core), tm: 4 (over y, x).
Axes of the slice: x: 2, y: 2, z: 4, core: 2. Of those that a mesh axis runs over, the one named last changes fastest.
Arguments:
- student_in: bfloat16 [8, 2048, 512], P('read', 'tm'), may hold values from -6 to 6
- teacher_rows: bfloat16 [8, 2048, 768], P('read', 'tm'), may hold values from -6 to 6
- valid: int32 [8], P('read'), may hold values from 512 to 2048, as said below
- conv_weight: bfloat16 [4, 3, 512, 512], replicated, may hold values from -0.15625 to 0.15625
- head_weight: bfloat16 [512, 5120], replicated, may hold values from -0.25 to 0.25
- teacher_head_weight: bfloat16 [768, 5120], replicated, may hold values from -0.21875 to 0.21875
Outputs:
- grad_conv: float32 [4, 3, 512, 512], P(None, None, 'read', 'tm')
- grad_head: float32 [512, 5120], P('read', 'tm')
The draws below stay inside these ranges and needn't reach their ends.
Inputs may be any that keep to these rules, and one draw needn't show every extreme that they name: One read of each draw has all 2048 frames valid.
All inputs are finite; a program needn't handle non-finite values.
Results may differ from the reference program's by a relative error of at most 0.002.
Values may be sent and summed in bfloat16 or wider, within the bound.
A program may use at most 192 MiB of HBM per device.

```python
import math
import jax
import jax.numpy as jnp
from jax import lax

D = 512
V = 5120
TE = 768
LAYERS = 4
BASE_DILATION = 32
FRAMES = 2048
READS = 8


def draw_valid(key, part):
    lengths = jax.random.randint(key, (READS,), FRAMES // 4, FRAMES + 1)
    position = jax.random.randint(jax.random.fold_in(key, 7), (), 0, READS)
    return lengths.at[position].set(FRAMES).astype(jnp.int32)


def level_of(key, dims, shards, low, high):
    factor_of, own = 1.0, jax.random.fold_in(key, 6)
    for dim, shards_of in shards:
        heights = jnp.exp(jax.random.uniform(jax.random.fold_in(own, dim), (shards_of,), jnp.float32, low / len(shards), high / len(shards)))
        factor_of = factor_of * jnp.repeat(heights, dims[dim] // shards_of).reshape([-1 if axis == dim else 1 for axis in range(len(dims))])
    return factor_of


def normal_values(key, shape, deviation, bound, split=(), held_as=jnp.bfloat16):
    level = level_of(key, shape, split, -0.22, 0.18) if split else 1.0
    entries = jax.random.normal(key, shape, jnp.float32) * deviation * level
    return jnp.minimum(jnp.maximum(entries, -bound), bound).astype(held_as)


def setup_inputs(seed: int = 0) -> dict:
    keys = jax.random.split(jax.random.key(seed), 7)
    return {
        "student_in": normal_values(keys[0], (READS, FRAMES, D), 1.0, 6.0, ((0, 8), (1, 4))),
        "teacher_rows": normal_values(keys[1], (READS, FRAMES, TE), 1.0, 6.0, ((0, 8), (1, 4))),
        "valid": draw_valid(jax.random.fold_in(keys[6], 71), 0),
        "conv_weight": normal_values(keys[3], (LAYERS, 3, D, D), (3 * D) ** -0.5, 0.15625),
        "head_weight": normal_values(keys[4], (D, V), D ** -0.5, 0.25),
        "teacher_head_weight": normal_values(keys[5], (TE, V), TE ** -0.5, 0.21875),
    }


def convolved_rows(hidden, weight, receptive_reach, frames):
    padded = jnp.pad(hidden, ((receptive_reach, receptive_reach), (0, 0)))
    total = jnp.zeros((frames, weight.shape[2]), jnp.float32)
    for tap_index in range(3):
        start = tap_index * receptive_reach
        total = total + jnp.dot(padded[start:start + frames], weight[tap_index], preferred_element_type=jnp.float32)
    return (padded, total)

def one_read(student_one, teacher_one, valid_one, conv_weight, head_weight, teacher_head_weight, loss_scale):
    frames = student_one.shape[0]
    signal_frame_mask = (jnp.arange(frames) < valid_one).astype(jnp.float32)[:, None]
    hidden = student_one
    saved = []
    for layer_number in range(LAYERS):
        receptive_reach = BASE_DILATION * 2 ** layer_number
        padded, pre = convolved_rows(hidden, conv_weight[layer_number], receptive_reach, frames)
        saved.append((padded, pre, receptive_reach))
        hidden = (signal_frame_mask * (hidden.astype(jnp.float32) + jax.nn.silu(pre))).astype(jnp.bfloat16)
    student_sum = jnp.dot(hidden, head_weight, preferred_element_type=jnp.float32)
    squash = jnp.tanh(student_sum)
    student = 5.0 * squash
    teacher = 5.0 * jnp.tanh(jnp.dot(teacher_one, teacher_head_weight, preferred_element_type=jnp.float32))
    prob_teacher = jax.nn.softmax(teacher, axis=-1)
    prob_student = jax.nn.softmax(student, axis=-1)
    g_score = (loss_scale * signal_frame_mask * (prob_student - prob_teacher) * 5.0 * (1.0 - squash * squash)).astype(jnp.bfloat16)
    grad_head = jnp.dot(hidden.T, g_score, preferred_element_type=jnp.float32)
    g_hidden = jnp.dot(g_score, head_weight.T, preferred_element_type=jnp.float32)
    grads = []
    for layer_number in reversed(range(LAYERS)):
        padded, pre, receptive_reach = saved[layer_number]
        g_act = signal_frame_mask * g_hidden
        sigma = jax.nn.sigmoid(pre)
        g_pre = (g_act * sigma * (1.0 + pre * (1.0 - sigma))).astype(jnp.bfloat16)
        taps = []
        for tap_index in range(3):
            start = tap_index * receptive_reach
            taps.append(jnp.dot(padded[start:start + frames].T, g_pre, preferred_element_type=jnp.float32))
        grads.append(jnp.stack(taps))
        if layer_number > 0:
            g_padded = jnp.pad(g_pre, ((receptive_reach, receptive_reach), (0, 0)))
            total = g_act
            for tap_index in range(3):
                start = (2 - tap_index) * receptive_reach
                total = total + jnp.dot(g_padded[start:start + frames], conv_weight[layer_number, tap_index].T, preferred_element_type=jnp.float32)
            g_hidden = total
    grad_conv = jnp.stack(grads[::-1])
    return (grad_conv, grad_head)

def reference(student_in, teacher_rows, valid, conv_weight, head_weight, teacher_head_weight):
    loss_scale = V / (3.0 * math.sqrt(READS * FRAMES))

    def distill_step_read(carry, items):
        student_one, teacher_one, valid_one = items
        grad_conv, grad_head = one_read(student_one, teacher_one, valid_one, conv_weight, head_weight, teacher_head_weight, loss_scale)
        return ((carry[0] + grad_conv, carry[1] + grad_head), None)
    start = (jnp.zeros((LAYERS, 3, D, D), jnp.float32), jnp.zeros((D, V), jnp.float32))
    totals, unused = lax.scan(distill_step_read, start, (student_in, teacher_rows, valid))
    return (totals[0], totals[1])
```

```python
import functools
import math

import jax
import jax.numpy as jnp
from jax import lax
from jax.experimental import pallas as pl
from jax.experimental.pallas import tpu as pltpu
from jax.sharding import PartitionSpec as P

LAYERS = 4
BASE_DILATION = 32
HEAD_GROUPS = 5
MESH = pl.DeviceIdType.MESH
BF16, F32 = jnp.bfloat16, jnp.float32


def reach(layer):
    return BASE_DILATION * 2**layer


def extended(x, width):
    devices, length = (lax.axis_size("tm"), x.shape[0])
    up = [(i, (i + 1) % devices) for i in range(devices - 1)]
    down = [(j, i) for i, j in up]
    before = lax.ppermute(x[length - width :], "tm", up)
    after = lax.ppermute(x[:width], "tm", down)
    return jnp.concatenate([before, x, after], axis=0)


def dot_tn(a, b):
    return lax.dot_general(a, b, (((0,), (0,)), ((), ())), preferred_element_type=F32)


def dot_nt(a, b):
    return lax.dot_general(a, b, (((1,), (1,)), ((), ())), preferred_element_type=F32)


def backward_kernel(
    n_read,
    n_tm,
    hid_mine,
    hid_other,
    gs,
    hw,
    cw,
    pre0,
    pre1,
    pre2,
    pre3,
    mask,
    out_conv,
    out_head,
    hid_far,
    gs_far,
    grad,
    gpad0,
    gpad1,
    gpad2,
    gpad3,
    gp_far,
    send_h,
    recv_h,
    acc_h,
    last_h,
    send_c,
    recv_c,
    acc_c,
    last_c,
    hid_sem,
    gs_sem,
    gp_sem,
    halo_sem,
    two_sem,
    three_sem,
):
    pres = (pre0, pre1, pre2, pre3)
    gpads = (gpad0, gpad1, gpad2, gpad3)
    frames, scores = gs.shape
    width = cw.shape[-1]
    n_q = n_read // 2
    half = width // 2
    rows = width // n_read
    cols = scores // n_tm
    conv_cols = width // n_tm
    sub = cols // HEAD_GROUPS
    r, t = lax.axis_index("read"), lax.axis_index("tm")
    core, q = lax.rem(r, 2), r // 2
    twin = {"read": 2 * q + 1 - core}
    tm_peers = [{"tm": lax.rem(t + k, n_tm)} for k in range(1, n_tm)]
    q_next = [lax.rem(q + k, n_q) for k in range(1, n_q)]
    q_peers = [{"read": 2 * other + core} for other in q_next]

    barrier = pltpu.get_barrier_semaphore()
    peers = [twin] + tm_peers + q_peers
    for peer in peers:
        pl.semaphore_signal(barrier, inc=1, device_id=peer, device_id_type=MESH)
    pl.semaphore_wait(barrier, len(peers))

    sent = []

    def remote(src, dst, send_sem, recv_sem, peer):
        return pltpu.make_async_remote_copy(
            src_ref=src,
            dst_ref=dst,
            send_sem=send_sem,
            recv_sem=recv_sem,
            device_id=peer,
            device_id_type=MESH,
        )

    def start(*what):
        copy = remote(*what)
        copy.start()
        sent.append(copy)
        return copy

    hid_copy = start(hid_other, hid_far, hid_sem.at[0], hid_sem.at[1], twin)
    gs_copies = []
    for s in range(HEAD_GROUPS):
        for owner in range(n_tm):
            part = pl.ds(owner * cols + s * sub, sub)
            gs_copies.append(
                start(
                    gs.at[:, part],
                    gs_far.at[:, part],
                    gs_sem.at[0, s, owner],
                    gs_sem.at[1, s, owner],
                    twin,
                )
            )

    step = scores // HEAD_GROUPS
    for s in range(HEAD_GROUPS):
        part = dot_nt(gs[:, s * step : (s + 1) * step], hw[:, s * step : (s + 1) * step])
        grad[...] = part if s == 0 else grad[...] + part

    gp_copies = {}
    two = {}
    three = {}
    halos = {}

    def make_gpre(layer):
        d = reach(layer)
        gpad, pre = gpads[layer], pres[layer][...]
        sigma = 1.0 / (1.0 + jnp.exp(-pre))
        g_act = mask[...] * grad[...]
        grad[...] = g_act
        gpad[d : d + frames, :] = (g_act * sigma * (1.0 + pre * (1.0 - sigma))).astype(BF16)
        if layer > 0:
            before = remote(
                gpad.at[pl.ds(d, d)],
                gpad.at[pl.ds(d + frames, d)],
                halo_sem.at[0, 0, layer],
                halo_sem.at[0, 1, layer],
                {"tm": lax.rem(t + n_tm - 1, n_tm)},
            )
            after = remote(
                gpad.at[pl.ds(frames, d)],
                gpad.at[pl.ds(0, d)],
                halo_sem.at[1, 0, layer],
                halo_sem.at[1, 1, layer],
                {"tm": lax.rem(t + 1, n_tm)},
            )
            halos[layer] = (before, after)

            @pl.when(t > 0)
            def _():
                before.start()

            @pl.when(t < n_tm - 1)
            def _():
                after.start()

            @pl.when(t == 0)
            def _():
                gpad[0:d, :] = jnp.zeros((d, width), BF16)

            @pl.when(t == n_tm - 1)
            def _():
                gpad[d + frames : d + frames + d, :] = jnp.zeros((d, width), BF16)

        gp_copies[layer] = start(
            gpad.at[pl.ds(d, frames)],
            gp_far.at[layer],
            gp_sem.at[0, layer],
            gp_sem.at[1, layer],
            twin,
        )

    def back(layer):
        d = reach(layer)
        gpad = gpads[layer]
        grad[...] = grad[...] + dot_nt(gpad[d : d + frames, :], cw[layer, 1])
        before, after = halos[layer]

        @pl.when(t < n_tm - 1)
        def _():
            before.wait_recv()

        @pl.when(t > 0)
        def _():
            after.wait_recv()

        grad[...] = grad[...] + dot_nt(gpad[2 * d : 2 * d + frames, :], cw[layer, 0])
        grad[...] = grad[...] + dot_nt(gpad[0:frames, :], cw[layer, 2])

        @pl.when(t > 0)
        def _():
            before.wait_send()

        @pl.when(t < n_tm - 1)
        def _():
            after.wait_send()

    def send_two(group, send_ref, recv_ref):
        two[group] = [
            start(
                send_ref.at[lax.rem(t + k, n_tm)],
                recv_ref.at[k - 1],
                two_sem.at[0, group, k - 1],
                two_sem.at[1, group, k - 1],
                tm_peers[k - 1],
            )
            for k in range(1, n_tm)
        ]

    hid_rows = sum(frames + 2 * reach(l) for l in range(LAYERS))

    def head(s):
        for owner in range(n_tm):
            gs_copies[s * n_tm + owner].wait_recv()
            at = owner * cols + s * sub
            total = dot_tn(hid_mine[hid_rows : hid_rows + frames, :], gs[:, at : at + sub])
            total = total + dot_tn(hid_far[hid_rows : hid_rows + frames, :], gs_far[:, at : at + sub])
            send_h[s, owner] = total.astype(BF16)

            @pl.when(t == owner)
            def _():
                acc_h[s] = total

        send_two(LAYERS + s, send_h.at[s], recv_h.at[s])

    def conv(layer):
        gp_copies[layer].wait_recv()
        d = reach(layer)
        base = sum(frames + 2 * reach(l) for l in range(layer))
        for k in range(3):
            at = base + k * d
            total = dot_tn(hid_mine[at : at + frames, :], gpads[layer][d : d + frames, :])
            total = total + dot_tn(hid_far[at : at + frames, :], gp_far[layer])
            for owner in range(n_tm):
                chunk = total[:, owner * conv_cols : (owner + 1) * conv_cols]
                send_c[layer, owner, k] = chunk.astype(BF16)

                @pl.when(t == owner)
                def _():
                    acc_c[layer, k] = chunk

        send_two(layer, send_c.at[layer], recv_c.at[layer])

    def finish_two(group):
        for copy in two[group]:
            copy.wait_recv()
        if group < LAYERS:
            for k in range(3):
                total = acc_c[group, k]
                for slot in range(n_tm - 1):
                    total = total + recv_c[group, slot, k].astype(F32)
                acc_c[group, k] = total
        else:
            total = acc_h[group - LAYERS]
            for slot in range(n_tm - 1):
                total = total + recv_h[group - LAYERS, slot].astype(F32)
            acc_h[group - LAYERS] = total
        three[group] = []
        for k in range(1, n_q):
            part = pl.ds(pl.multiple_of(q_next[k - 1] * rows, rows), rows)
            if group < LAYERS:
                src, dst = acc_c.at[group, :, part], last_c.at[group, k - 1]
            else:
                src, dst = acc_h.at[group - LAYERS, part], last_h.at[group - LAYERS, k - 1]
            three[group].append(
                start(
                    src,
                    dst,
                    three_sem.at[0, group, k - 1],
                    three_sem.at[1, group, k - 1],
                    q_peers[k - 1],
                )
            )

    def finish_three(group):
        for copy in three[group]:
            copy.wait_recv()
        part = pl.ds(pl.multiple_of(q * rows, rows), rows)
        if group < LAYERS:
            for k in range(3):
                total = acc_c[group, k, part, :]
                for slot in range(n_q - 1):
                    total = total + last_c[group, slot, k]
                out_conv[group, k] = total
        else:
            s = group - LAYERS
            total = acc_h[s, part, :]
            for slot in range(n_q - 1):
                total = total + last_h[s, slot]
            out_head[:, s * sub : (s + 1) * sub] = total

    make_gpre(3)
    hid_copy.wait_recv()
    head(0)
    head(1)
    back(3)
    make_gpre(2)
    head(2)
    head(3)
    back(2)
    make_gpre(1)
    head(4)
    conv(3)
    finish_two(4)
    back(1)
    make_gpre(0)
    conv(2)
    finish_two(5)
    conv(1)
    finish_two(6)
    conv(0)
    finish_two(7)
    finish_two(8)
    finish_three(4)
    finish_two(3)
    finish_three(5)
    finish_two(2)
    finish_three(6)
    finish_three(7)
    finish_two(1)
    finish_three(8)
    finish_two(0)
    for group in (3, 2, 1, 0):
        finish_three(group)
    for copy in sent:
        copy.wait_send()


def backward(hid_mine, hid_other, gs, hw, cw, pres, mask):
    n_read, n_tm = lax.axis_size("read"), lax.axis_size("tm")
    frames, scores = gs.shape
    width = cw.shape[-1]
    n_q, half, rows = n_read // 2, width // 2, width // n_read
    cols, conv_cols = scores // n_tm, width // n_tm
    sub = cols // HEAD_GROUPS
    groups = LAYERS + HEAD_GROUPS
    vmem = pl.BlockSpec(memory_space=pltpu.VMEM)
    dma = pltpu.SemaphoreType.DMA
    return pl.pallas_call(
        functools.partial(backward_kernel, n_read, n_tm),
        out_shape=(
            jax.ShapeDtypeStruct((LAYERS, 3, rows, conv_cols), F32),
            jax.ShapeDtypeStruct((rows, cols), F32),
        ),
        in_specs=[vmem] * 10,
        out_specs=(vmem, vmem),
        scratch_shapes=[
            pltpu.VMEM(hid_mine.shape, BF16),
            pltpu.VMEM((frames, scores), BF16),
            pltpu.VMEM((frames, width), F32),
        ]
        + [pltpu.VMEM((frames + 2 * reach(l), width), BF16) for l in range(LAYERS)]
        + [
            pltpu.VMEM((LAYERS, frames, width), BF16),
            pltpu.VMEM((HEAD_GROUPS, n_tm, half, sub), BF16),
            pltpu.VMEM((HEAD_GROUPS, n_tm - 1, half, sub), BF16),
            pltpu.VMEM((HEAD_GROUPS, half, sub), F32),
            pltpu.VMEM((HEAD_GROUPS, n_q - 1, rows, sub), F32),
            pltpu.VMEM((LAYERS, n_tm, 3, half, conv_cols), BF16),
            pltpu.VMEM((LAYERS, n_tm - 1, 3, half, conv_cols), BF16),
            pltpu.VMEM((LAYERS, 3, half, conv_cols), F32),
            pltpu.VMEM((LAYERS, n_q - 1, 3, rows, conv_cols), F32),
            dma((2,)),
            dma((2, HEAD_GROUPS, n_tm)),
            dma((2, LAYERS)),
            dma((2, 2, LAYERS)),
            dma((2, groups, n_tm - 1)),
            dma((2, groups, n_q - 1)),
        ],
        compiler_params=pltpu.CompilerParams(
            collective_id=1, has_side_effects=True, vmem_limit_bytes=60 * 2**20
        ),
    )(hid_mine, hid_other, gs, hw, cw, *pres, mask)


def on_device(student_in, teacher_rows, valid, conv_weight, head_weight, teacher_head_weight):
    reads_dev, frames, width = student_in.shape
    n_read = lax.axis_size("read")
    scores = head_weight.shape[1]
    loss_scale = scores / (
        3.0 * math.sqrt(reads_dev * n_read * frames * lax.axis_size("tm"))
    )
    first_frame = lax.axis_index("tm") * frames
    positions = first_frame + jnp.arange(frames, dtype=jnp.int32)
    mask = (positions < valid[0]).astype(F32)[:, None]
    hidden = student_in[0]
    pads, pres = [], []
    for layer in range(LAYERS):
        d = reach(layer)
        padded = extended(hidden, d)
        pre = jnp.zeros((frames, width), F32)
        for k in range(3):
            pre = pre + jnp.dot(
                padded[k * d : k * d + frames], conv_weight[layer, k], preferred_element_type=F32
            )
        pads.append(padded)
        pres.append(pre)
        hidden = (mask * (hidden.astype(F32) + jax.nn.silu(pre))).astype(BF16)
    squash = jnp.tanh(jnp.dot(hidden, head_weight, preferred_element_type=F32))
    teacher = 5.0 * jnp.tanh(
        jnp.dot(teacher_rows[0], teacher_head_weight, preferred_element_type=F32)
    )
    prob_teacher = jax.nn.softmax(teacher, axis=-1)
    prob_student = jax.nn.softmax(5.0 * squash, axis=-1)
    g_score = (
        loss_scale * mask * (prob_student - prob_teacher) * 5.0 * (1.0 - squash * squash)
    ).astype(BF16)
    every = jnp.concatenate(pads + [hidden], axis=0)
    every = every.reshape(every.shape[0], n_read // 2, 2, width // n_read)
    core = lax.rem(lax.axis_index("read"), 2)
    mine, other = (
        lax.dynamic_index_in_dim(every, which, 2, keepdims=False).reshape(-1, width // 2)
        for which in (core, 1 - core)
    )
    return backward(mine, other, g_score, head_weight, conv_weight, pres, mask)


def solution(mesh):
    return jax.shard_map(
        on_device,
        mesh=mesh,
        in_specs=(P("read", "tm", None), P("read", "tm", None), P("read"), P(), P(), P()),
        out_specs=(P(None, None, "read", "tm"), P("read", "tm")),
        check_vma=False,
    )
```

```python
import functools
import math

import jax
import jax.numpy as jnp
from jax import lax
from jax.experimental import pallas as pl
from jax.experimental.pallas import tpu as pltpu
from jax.sharding import PartitionSpec as P

LAYERS = 4
BASE_DILATION = 32
HEAD_GROUPS = 5
MESH = pl.DeviceIdType.MESH
BF16, F32 = jnp.bfloat16, jnp.float32


def reach(layer):
    return BASE_DILATION * 2**layer


def dot_tn(a, b):
    return lax.dot_general(a, b, (((0,), (0,)), ((), ())), preferred_element_type=F32)


def dot_nt(a, b):
    return lax.dot_general(a, b, (((1,), (1,)), ((), ())), preferred_element_type=F32)


def backward_kernel(
    n_read,
    n_tm,
    hid_mine_hbm,
    hid_other,
    gs_hbm,
    hw_hbm,
    cw_hbm,
    pre0_hbm,
    pre1_hbm,
    pre2_hbm,
    pre3_hbm,
    mask,
    out_conv,
    out_head,
    hid_mine,
    gs,
    hw,
    cw,
    pre0,
    pre1,
    pre2,
    pre3,
    hid_far,
    gs_far,
    grad,
    gpad0,
    gpad1,
    gpad2,
    gpad3,
    gp_far,
    send_h,
    recv_h,
    acc_h,
    done_h,
    last_h,
    send_c,
    recv_c,
    acc_c,
    done_c,
    last_c,
    hid_sem,
    gs_sem,
    gp_sem,
    halo_sem,
    two_sem,
    three_sem,
    gs_load_sem,
    hw_load_sem,
    load_sem,
):
    pres = (pre0, pre1, pre2, pre3)
    gpads = (gpad0, gpad1, gpad2, gpad3)
    frames, scores = gs.shape
    width = cw.shape[-1]
    n_q = n_read // 2
    half = width // 2
    rows = width // n_read
    cols = scores // n_tm
    conv_cols = width // n_tm
    sub = cols // HEAD_GROUPS
    r, t = lax.axis_index("read"), lax.axis_index("tm")
    core, q = lax.rem(r, 2), r // 2
    step = scores // HEAD_GROUPS
    gs_loads, hw_loads = [], []
    for s in range(HEAD_GROUPS):
        part = pl.ds(s * step, step)
        for loads, far, near, sem in (
            (gs_loads, gs_hbm, gs, gs_load_sem),
            (hw_loads, hw_hbm, hw, hw_load_sem),
        ):
            loads.append(pltpu.make_async_copy(far.at[:, part], near.at[:, part], sem.at[s]))
            loads[-1].start()
    pre_hbm = (pre0_hbm, pre1_hbm, pre2_hbm, pre3_hbm)
    pre_loads = [
        pltpu.make_async_copy(pre_hbm[l], pres[l], load_sem.at[l]) for l in range(LAYERS)
    ]
    hid_load = pltpu.make_async_copy(hid_mine_hbm, hid_mine, load_sem.at[LAYERS])
    cw_load = pltpu.make_async_copy(cw_hbm.at[pl.ds(1, LAYERS - 1)], cw, load_sem.at[LAYERS + 1])
    for load in (pre_loads[3], hid_load, cw_load, pre_loads[2], pre_loads[1], pre_loads[0]):
        load.start()
    twin = {"read": 2 * q + 1 - core}
    tm_peers = [{"tm": lax.rem(t + k, n_tm)} for k in range(1, n_tm)]
    q_next = [lax.rem(q + k, n_q) for k in range(1, n_q)]
    q_peers = [{"read": 2 * other + core} for other in q_next]

    barrier = pltpu.get_barrier_semaphore()
    peers = [twin] + tm_peers + q_peers
    for peer in peers:
        pl.semaphore_signal(barrier, inc=1, device_id=peer, device_id_type=MESH)
    pl.semaphore_wait(barrier, len(peers))

    sent = []

    def remote(src, dst, send_sem, recv_sem, peer):
        return pltpu.make_async_remote_copy(
            src_ref=src,
            dst_ref=dst,
            send_sem=send_sem,
            recv_sem=recv_sem,
            device_id=peer,
            device_id_type=MESH,
        )

    def start(*what):
        copy = remote(*what)
        copy.start()
        sent.append(copy)
        return copy

    hid_copy = start(hid_other, hid_far, hid_sem.at[0], hid_sem.at[1], twin)
    gs_copies = []
    for s in range(HEAD_GROUPS):
        for owner in range(n_tm):
            part = pl.ds(owner * cols + s * sub, sub)
            gs_copies.append(
                start(
                    gs_hbm.at[:, part],
                    gs_far.at[:, part],
                    gs_sem.at[0, s, owner],
                    gs_sem.at[1, s, owner],
                    twin,
                )
            )

    for s in range(HEAD_GROUPS):
        gs_loads[s].wait()
        hw_loads[s].wait()
        part = dot_nt(gs[:, s * step : (s + 1) * step], hw[:, s * step : (s + 1) * step])
        grad[...] = part if s == 0 else grad[...] + part

    gp_copies = {}
    two = {}
    three = {}
    halos = {}

    def make_gpre(layer):
        d = reach(layer)
        pre_loads[layer].wait()
        gpad, pre = gpads[layer], pres[layer][...]
        sigma = 1.0 / (1.0 + jnp.exp(-pre))
        g_act = mask[...] * grad[...]
        grad[...] = g_act
        gpad[d : d + frames, :] = (g_act * sigma * (1.0 + pre * (1.0 - sigma))).astype(BF16)
        if layer > 0:
            before = remote(
                gpad.at[pl.ds(d, d)],
                gpad.at[pl.ds(d + frames, d)],
                halo_sem.at[0, 0, layer],
                halo_sem.at[0, 1, layer],
                {"tm": lax.rem(t + n_tm - 1, n_tm)},
            )
            after = remote(
                gpad.at[pl.ds(frames, d)],
                gpad.at[pl.ds(0, d)],
                halo_sem.at[1, 0, layer],
                halo_sem.at[1, 1, layer],
                {"tm": lax.rem(t + 1, n_tm)},
            )
            halos[layer] = (before, after)

            @pl.when(t > 0)
            def _():
                before.start()

            @pl.when(t < n_tm - 1)
            def _():
                after.start()

            @pl.when(t == 0)
            def _():
                gpad[0:d, :] = jnp.zeros((d, width), BF16)

            @pl.when(t == n_tm - 1)
            def _():
                gpad[d + frames : d + frames + d, :] = jnp.zeros((d, width), BF16)

        gp_copies[layer] = start(
            gpad.at[pl.ds(d, frames)],
            gp_far.at[layer],
            gp_sem.at[0, layer],
            gp_sem.at[1, layer],
            twin,
        )

    def back(layer):
        d = reach(layer)
        gpad = gpads[layer]
        grad[...] = grad[...] + dot_nt(gpad[d : d + frames, :], cw[layer - 1, 1])
        before, after = halos[layer]

        @pl.when(t < n_tm - 1)
        def _():
            before.wait_recv()

        @pl.when(t > 0)
        def _():
            after.wait_recv()

        grad[...] = grad[...] + dot_nt(gpad[2 * d : 2 * d + frames, :], cw[layer - 1, 0])
        grad[...] = grad[...] + dot_nt(gpad[0:frames, :], cw[layer - 1, 2])

        @pl.when(t > 0)
        def _():
            before.wait_send()

        @pl.when(t < n_tm - 1)
        def _():
            after.wait_send()

    def send_two(group, send_ref, recv_ref):
        two[group] = [
            start(
                send_ref.at[lax.rem(t + k, n_tm)],
                recv_ref.at[k - 1],
                two_sem.at[0, group, k - 1],
                two_sem.at[1, group, k - 1],
                tm_peers[k - 1],
            )
            for k in range(1, n_tm)
        ]

    hid_rows = sum(frames + 2 * reach(l) for l in range(LAYERS))

    def head(s):
        for owner in range(n_tm):
            gs_copies[s * n_tm + owner].wait_recv()
            at = owner * cols + s * sub
            total = dot_tn(hid_mine[hid_rows : hid_rows + frames, :], gs[:, at : at + sub])
            total = total + dot_tn(hid_far[hid_rows : hid_rows + frames, :], gs_far[:, at : at + sub])
            send_h[s, owner] = total.astype(BF16)

            @pl.when(t == owner)
            def _():
                acc_h[s] = total

        send_two(LAYERS + s, send_h.at[s], recv_h.at[s])

    def conv(layer):
        gp_copies[layer].wait_recv()
        d = reach(layer)
        base = sum(frames + 2 * reach(l) for l in range(layer))
        for k in range(3):
            at = base + k * d
            total = dot_tn(hid_mine[at : at + frames, :], gpads[layer][d : d + frames, :])
            total = total + dot_tn(hid_far[at : at + frames, :], gp_far[layer])
            for owner in range(n_tm):
                chunk = total[:, owner * conv_cols : (owner + 1) * conv_cols]
                send_c[layer, owner, k] = chunk.astype(BF16)

                @pl.when(t == owner)
                def _():
                    acc_c[layer, k] = chunk

        send_two(layer, send_c.at[layer], recv_c.at[layer])

    def finish_two(group):
        for copy in two[group]:
            copy.wait_recv()
        if group < LAYERS:
            for k in range(3):
                total = acc_c[group, k]
                for slot in range(n_tm - 1):
                    total = total + recv_c[group, slot, k].astype(F32)
                acc_c[group, k] = total
                done_c[group, k] = total.astype(BF16)
        else:
            total = acc_h[group - LAYERS]
            for slot in range(n_tm - 1):
                total = total + recv_h[group - LAYERS, slot].astype(F32)
            acc_h[group - LAYERS] = total
            done_h[group - LAYERS] = total.astype(BF16)
        three[group] = []
        for k in range(1, n_q):
            part = pl.ds(pl.multiple_of(q_next[k - 1] * rows, rows), rows)
            if group < LAYERS:
                src, dst = done_c.at[group, :, part], last_c.at[group, k - 1]
            else:
                src, dst = done_h.at[group - LAYERS, part], last_h.at[group - LAYERS, k - 1]
            three[group].append(
                start(
                    src,
                    dst,
                    three_sem.at[0, group, k - 1],
                    three_sem.at[1, group, k - 1],
                    q_peers[k - 1],
                )
            )

    def finish_three(group):
        for copy in three[group]:
            copy.wait_recv()
        part = pl.ds(pl.multiple_of(q * rows, rows), rows)
        if group < LAYERS:
            for k in range(3):
                total = acc_c[group, k, part, :]
                for slot in range(n_q - 1):
                    total = total + last_c[group, slot, k].astype(F32)
                out_conv[group, k] = total
        else:
            s = group - LAYERS
            total = acc_h[s, part, :]
            for slot in range(n_q - 1):
                total = total + last_h[s, slot].astype(F32)
            out_head[:, s * sub : (s + 1) * sub] = total

    make_gpre(3)
    hid_load.wait()
    hid_copy.wait_recv()
    head(0)
    head(1)
    cw_load.wait()
    back(3)
    make_gpre(2)
    head(2)
    head(3)
    back(2)
    make_gpre(1)
    head(4)
    conv(3)
    finish_two(4)
    back(1)
    make_gpre(0)
    conv(2)
    finish_two(5)
    conv(1)
    finish_two(6)
    conv(0)
    finish_two(7)
    finish_two(8)
    finish_three(4)
    finish_two(3)
    finish_three(5)
    finish_two(2)
    finish_three(6)
    finish_three(7)
    finish_two(1)
    finish_three(8)
    finish_two(0)
    for group in (3, 2, 1, 0):
        finish_three(group)
    for copy in sent:
        copy.wait_send()


def backward(hid_mine, hid_other, gs, hw, cw, pres, mask):
    n_read, n_tm = lax.axis_size("read"), lax.axis_size("tm")
    frames, scores = gs.shape
    width = cw.shape[-1]
    n_q, half, rows = n_read // 2, width // 2, width // n_read
    cols, conv_cols = scores // n_tm, width // n_tm
    sub = cols // HEAD_GROUPS
    groups = LAYERS + HEAD_GROUPS
    vmem = pl.BlockSpec(memory_space=pltpu.VMEM)
    dma = pltpu.SemaphoreType.DMA
    return pl.pallas_call(
        functools.partial(backward_kernel, n_read, n_tm),
        out_shape=(
            jax.ShapeDtypeStruct((LAYERS, 3, rows, conv_cols), F32),
            jax.ShapeDtypeStruct((rows, cols), F32),
        ),
        in_specs=[pl.BlockSpec(memory_space=pl.ANY)] * 9 + [vmem],
        out_specs=(vmem, vmem),
        scratch_shapes=[
            pltpu.VMEM(hid_mine.shape, BF16),
            pltpu.VMEM(gs.shape, BF16),
            pltpu.VMEM(hw.shape, BF16),
            pltpu.VMEM((LAYERS - 1,) + cw.shape[1:], BF16),
        ]
        + [pltpu.VMEM((frames, width), F32)] * LAYERS
        + [
            pltpu.VMEM(hid_mine.shape, BF16),
            pltpu.VMEM((frames, scores), BF16),
            pltpu.VMEM((frames, width), F32),
        ]
        + [pltpu.VMEM((frames + 2 * reach(l), width), BF16) for l in range(LAYERS)]
        + [
            pltpu.VMEM((LAYERS, frames, width), BF16),
            pltpu.VMEM((HEAD_GROUPS, n_tm, half, sub), BF16),
            pltpu.VMEM((HEAD_GROUPS, n_tm - 1, half, sub), BF16),
            pltpu.VMEM((HEAD_GROUPS, half, sub), F32),
            pltpu.VMEM((HEAD_GROUPS, half, sub), BF16),
            pltpu.VMEM((HEAD_GROUPS, n_q - 1, rows, sub), BF16),
            pltpu.VMEM((LAYERS, n_tm, 3, half, conv_cols), BF16),
            pltpu.VMEM((LAYERS, n_tm - 1, 3, half, conv_cols), BF16),
            pltpu.VMEM((LAYERS, 3, half, conv_cols), F32),
            pltpu.VMEM((LAYERS, 3, half, conv_cols), BF16),
            pltpu.VMEM((LAYERS, n_q - 1, 3, rows, conv_cols), BF16),
            dma((2,)),
            dma((2, HEAD_GROUPS, n_tm)),
            dma((2, LAYERS)),
            dma((2, 2, LAYERS)),
            dma((2, groups, n_tm - 1)),
            dma((2, groups, n_q - 1)),
            dma((HEAD_GROUPS,)),
            dma((HEAD_GROUPS,)),
            dma((LAYERS + 2,)),
        ],
        compiler_params=pltpu.CompilerParams(
            collective_id=1, has_side_effects=True, vmem_limit_bytes=60 * 2**20
        ),
    )(hid_mine, hid_other, gs, hw, cw, *pres, mask)


def forward_kernel(
    n_read,
    n_tm,
    x,
    cw_hbm,
    mask,
    out_mine,
    out_other,
    out_hidden,
    pre0,
    pre1,
    pre2,
    pre3,
    hp0,
    hp1,
    hp2,
    hp3,
    cw,
    cw_sem,
    halo_sem,
):
    pres, pads = (pre0, pre1, pre2, pre3), (hp0, hp1, hp2, hp3)
    frames, width = x.shape
    half, rows = width // 2, width // n_read
    r, t = lax.axis_index("read"), lax.axis_index("tm")
    core = lax.rem(r, 2)
    loads = [
        pltpu.make_async_copy(cw_hbm.at[l], cw.at[l], cw_sem.at[l]) for l in range(LAYERS)
    ]
    for load in loads:
        load.start()
    hp0[reach(0) : reach(0) + frames, :] = x[...]

    barrier = pltpu.get_barrier_semaphore()
    for k in range(1, n_tm):
        pl.semaphore_signal(
            barrier, inc=1, device_id={"tm": lax.rem(t + k, n_tm)}, device_id_type=MESH
        )
    pl.semaphore_wait(barrier, n_tm - 1)

    channel = lax.broadcasted_iota(jnp.int32, (width, half), 0)
    place = lax.broadcasted_iota(jnp.int32, (width, half), 1)
    wanted = 2 * rows * (place // rows) + lax.rem(place, rows)
    pick_mine = (channel == wanted + rows * core).astype(F32).astype(BF16)
    pick_other = (channel == wanted + rows * (1 - core)).astype(F32).astype(BF16)

    def deal(value, at):
        size = value.shape[0]
        for out, pick in ((out_mine, pick_mine), (out_other, pick_other)):
            out[at : at + size, :] = jnp.dot(
                value, pick, preferred_element_type=F32
            ).astype(BF16)

    base = 0
    for layer in range(LAYERS):
        d = reach(layer)
        pad = pads[layer]

        def halo(side, first, landing, to, pad=pad, d=d, layer=layer):
            return pltpu.make_async_remote_copy(
                src_ref=pad.at[pl.ds(first, d)],
                dst_ref=pad.at[pl.ds(landing, d)],
                send_sem=halo_sem.at[side, 0, layer],
                recv_sem=halo_sem.at[side, 1, layer],
                device_id={"tm": lax.rem(t + to, n_tm)},
                device_id_type=MESH,
            )

        before = halo(0, d, d + frames, n_tm - 1)
        after = halo(1, frames, 0, 1)

        @pl.when(t > 0)
        def _():
            before.start()

        @pl.when(t < n_tm - 1)
        def _():
            after.start()

        @pl.when(t == 0)
        def _():
            pad[0:d, :] = jnp.zeros((d, width), BF16)

        @pl.when(t == n_tm - 1)
        def _():
            pad[d + frames : d + frames + d, :] = jnp.zeros((d, width), BF16)

        loads[layer].wait()
        pre = pres[layer]
        pre[...] = jnp.dot(pad[d : d + frames, :], cw[layer, 1], preferred_element_type=F32)
        deal(pad[d : d + frames, :], base + d)

        @pl.when(t < n_tm - 1)
        def _():
            before.wait_recv()

        @pl.when(t > 0)
        def _():
            after.wait_recv()

        pre[...] += jnp.dot(pad[0:frames, :], cw[layer, 0], preferred_element_type=F32)
        pre[...] += jnp.dot(
            pad[2 * d : 2 * d + frames, :], cw[layer, 2], preferred_element_type=F32
        )
        total = pre[...]
        hidden = (
            mask[...]
            * (pad[d : d + frames, :].astype(F32) + total * (1.0 / (1.0 + jnp.exp(-total))))
        ).astype(BF16)
        if layer < LAYERS - 1:
            pads[layer + 1][2 * d : 2 * d + frames, :] = hidden
        else:
            out_hidden[...] = hidden
        deal(pad[0:d, :], base)
        deal(pad[d + frames : d + frames + d, :], base + d + frames)

        @pl.when(t > 0)
        def _():
            before.wait_send()

        @pl.when(t < n_tm - 1)
        def _():
            after.wait_send()

        base += frames + 2 * d
    deal(out_hidden[...], base)


def forward(x, cw, mask):
    n_read, n_tm = lax.axis_size("read"), lax.axis_size("tm")
    frames, width = x.shape
    total = frames + sum(frames + 2 * reach(l) for l in range(LAYERS))
    vmem = pl.BlockSpec(memory_space=pltpu.VMEM)
    dma = pltpu.SemaphoreType.DMA
    return pl.pallas_call(
        functools.partial(forward_kernel, n_read, n_tm),
        out_shape=[
            jax.ShapeDtypeStruct((total, width // 2), BF16),
            jax.ShapeDtypeStruct((total, width // 2), BF16),
            jax.ShapeDtypeStruct((frames, width), BF16),
        ]
        + [jax.ShapeDtypeStruct((frames, width), F32)] * LAYERS,
        in_specs=[vmem, pl.BlockSpec(memory_space=pl.ANY), vmem],
        out_specs=[vmem] * (3 + LAYERS),
        scratch_shapes=[
            pltpu.VMEM((frames + 2 * reach(l), width), BF16) for l in range(LAYERS)
        ]
        + [pltpu.VMEM(cw.shape, BF16), dma((LAYERS,)), dma((2, 2, LAYERS))],
        compiler_params=pltpu.CompilerParams(
            collective_id=0, has_side_effects=True, vmem_limit_bytes=48 * 2**20
        ),
    )(x, cw, mask)


def on_device(student_in, teacher_rows, valid, conv_weight, head_weight, teacher_head_weight):
    reads_dev, frames, width = student_in.shape
    n_read = lax.axis_size("read")
    scores = head_weight.shape[1]
    loss_scale = scores / (
        3.0 * math.sqrt(reads_dev * n_read * frames * lax.axis_size("tm"))
    )
    first_frame = lax.axis_index("tm") * frames
    positions = first_frame + jnp.arange(frames, dtype=jnp.int32)
    mask = (positions < valid[0]).astype(F32)[:, None]
    mine, other, hidden, *pres = forward(student_in[0], conv_weight, mask)
    squash = jnp.tanh(jnp.dot(hidden, head_weight, preferred_element_type=F32))
    teacher = 5.0 * jnp.tanh(
        jnp.dot(teacher_rows[0], teacher_head_weight, preferred_element_type=F32)
    )
    prob_teacher = jax.nn.softmax(teacher, axis=-1)
    prob_student = jax.nn.softmax(5.0 * squash, axis=-1)
    g_score = (
        loss_scale * mask * (prob_student - prob_teacher) * 5.0 * (1.0 - squash * squash)
    ).astype(BF16)
    return backward(mine, other, g_score, head_weight, conv_weight, pres, mask)


def solution(mesh):
    return jax.shard_map(
        on_device,
        mesh=mesh,
        in_specs=(P("read", "tm", None), P("read", "tm", None), P("read"), P(), P(), P()),
        out_specs=(P(None, None, "read", "tm"), P("read", "tm")),
        check_vma=False,
    )
```

```python
import functools
import math

import jax
import jax.numpy as jnp
from jax import lax
from jax.experimental import pallas as pl
from jax.experimental.pallas import tpu as pltpu
from jax.sharding import PartitionSpec as P

LAYERS = 4
BASE_DILATION = 32
HEAD_GROUPS = 5
MESH = pl.DeviceIdType.MESH
BF16, F32 = jnp.bfloat16, jnp.float32


def reach(layer):
    return BASE_DILATION * 2**layer


def dot_tn(a, b):
    return lax.dot_general(a, b, (((0,), (0,)), ((), ())), preferred_element_type=F32)


def dot_nt(a, b):
    return lax.dot_general(a, b, (((1,), (1,)), ((), ())), preferred_element_type=F32)


def backward_kernel(
    n_read,
    n_tm,
    hid_mine_hbm,
    hid_other,
    gs_hbm,
    hw_hbm,
    cw_hbm,
    pre0_hbm,
    pre1_hbm,
    pre2_hbm,
    pre3_hbm,
    mask,
    out_conv,
    out_head,
    hid_mine,
    gs,
    hw,
    cw,
    pre0,
    pre1,
    pre2,
    pre3,
    hid_far,
    gs_far,
    grad,
    gpad0,
    gpad1,
    gpad2,
    gpad3,
    gp_far,
    send_h,
    recv_h,
    acc_h,
    done_h,
    last_h,
    send_c,
    recv_c,
    acc_c,
    done_c,
    last_c,
    hid_sem,
    gs_sem,
    gp_sem,
    halo_sem,
    two_sem,
    three_sem,
    gs_load_sem,
    hw_load_sem,
    load_sem,
):
    pres = (pre0, pre1, pre2, pre3)
    gpads = (gpad0, gpad1, gpad2, gpad3)
    frames, scores = gs.shape
    width = cw.shape[-1]
    n_q = n_read // 2
    half = width // 2
    rows = width // n_read
    cols = scores // n_tm
    conv_cols = width // n_tm
    sub = cols // HEAD_GROUPS
    r, t = lax.axis_index("read"), lax.axis_index("tm")
    core, q = lax.rem(r, 2), r // 2
    step = scores // HEAD_GROUPS
    gs_loads, hw_loads = [], []
    for s in range(HEAD_GROUPS):
        part = pl.ds(s * step, step)
        for loads, far, near, sem in (
            (gs_loads, gs_hbm, gs, gs_load_sem),
            (hw_loads, hw_hbm, hw, hw_load_sem),
        ):
            loads.append(pltpu.make_async_copy(far.at[:, part], near.at[:, part], sem.at[s]))
            loads[-1].start()
    pre_hbm = (pre0_hbm, pre1_hbm, pre2_hbm, pre3_hbm)
    pre_loads = [
        pltpu.make_async_copy(pre_hbm[l], pres[l], load_sem.at[l]) for l in range(LAYERS)
    ]
    hid_load = pltpu.make_async_copy(hid_mine_hbm, hid_mine, load_sem.at[LAYERS])
    cw_load = pltpu.make_async_copy(cw_hbm.at[pl.ds(1, LAYERS - 1)], cw, load_sem.at[LAYERS + 1])
    for load in (pre_loads[3], hid_load, cw_load, pre_loads[2], pre_loads[1], pre_loads[0]):
        load.start()
    twin = {"read": 2 * q + 1 - core}
    tm_peers = [{"tm": lax.rem(t + k, n_tm)} for k in range(1, n_tm)]
    q_next = [lax.rem(q + k, n_q) for k in range(1, n_q)]
    q_peers = [{"read": 2 * other + core} for other in q_next]

    barrier = pltpu.get_barrier_semaphore()
    peers = [twin] + tm_peers + q_peers
    for peer in peers:
        pl.semaphore_signal(barrier, inc=1, device_id=peer, device_id_type=MESH)
    pl.semaphore_wait(barrier, len(peers))

    sent = []

    def remote(src, dst, send_sem, recv_sem, peer):
        return pltpu.make_async_remote_copy(
            src_ref=src,
            dst_ref=dst,
            send_sem=send_sem,
            recv_sem=recv_sem,
            device_id=peer,
            device_id_type=MESH,
        )

    def start(*what):
        copy = remote(*what)
        copy.start()
        sent.append(copy)
        return copy

    hid_copy = start(hid_other, hid_far, hid_sem.at[0], hid_sem.at[1], twin)
    gs_copies = []
    for s in range(HEAD_GROUPS):
        for owner in range(n_tm):
            part = pl.ds(owner * cols + s * sub, sub)
            gs_copies.append(
                start(
                    gs_hbm.at[:, part],
                    gs_far.at[:, part],
                    gs_sem.at[0, s, owner],
                    gs_sem.at[1, s, owner],
                    twin,
                )
            )

    def head_back():
        for s in range(HEAD_GROUPS):
            hw_loads[s].wait()
            part = dot_nt(gs[:, s * step : (s + 1) * step], hw[:, s * step : (s + 1) * step])
            grad[...] = part if s == 0 else grad[...] + part

    gp_copies = {}
    two = {}
    three = {}
    halos = {}

    def make_gpre(layer):
        d = reach(layer)
        pre_loads[layer].wait()
        gpad, pre = gpads[layer], pres[layer][...]
        sigma = 1.0 / (1.0 + jnp.exp(-pre))
        g_act = mask[...] * grad[...]
        grad[...] = g_act
        gpad[d : d + frames, :] = (g_act * sigma * (1.0 + pre * (1.0 - sigma))).astype(BF16)
        if layer > 0:
            before = remote(
                gpad.at[pl.ds(d, d)],
                gpad.at[pl.ds(d + frames, d)],
                halo_sem.at[0, 0, layer],
                halo_sem.at[0, 1, layer],
                {"tm": lax.rem(t + n_tm - 1, n_tm)},
            )
            after = remote(
                gpad.at[pl.ds(frames, d)],
                gpad.at[pl.ds(0, d)],
                halo_sem.at[1, 0, layer],
                halo_sem.at[1, 1, layer],
                {"tm": lax.rem(t + 1, n_tm)},
            )
            halos[layer] = (before, after)

            @pl.when(t > 0)
            def _():
                before.start()

            @pl.when(t < n_tm - 1)
            def _():
                after.start()

            @pl.when(t == 0)
            def _():
                gpad[0:d, :] = jnp.zeros((d, width), BF16)

            @pl.when(t == n_tm - 1)
            def _():
                gpad[d + frames : d + frames + d, :] = jnp.zeros((d, width), BF16)

        gp_copies[layer] = start(
            gpad.at[pl.ds(d, frames)],
            gp_far.at[layer],
            gp_sem.at[0, layer],
            gp_sem.at[1, layer],
            twin,
        )

    def back(layer):
        d = reach(layer)
        gpad = gpads[layer]
        grad[...] = grad[...] + dot_nt(gpad[d : d + frames, :], cw[layer - 1, 1])
        before, after = halos[layer]

        @pl.when(t < n_tm - 1)
        def _():
            before.wait_recv()

        @pl.when(t > 0)
        def _():
            after.wait_recv()

        grad[...] = grad[...] + dot_nt(gpad[2 * d : 2 * d + frames, :], cw[layer - 1, 0])
        grad[...] = grad[...] + dot_nt(gpad[0:frames, :], cw[layer - 1, 2])

        @pl.when(t > 0)
        def _():
            before.wait_send()

        @pl.when(t < n_tm - 1)
        def _():
            after.wait_send()

    def send_two(group, send_ref, recv_ref):
        two[group] = [
            start(
                send_ref.at[lax.rem(t + k, n_tm)],
                recv_ref.at[k - 1],
                two_sem.at[0, group, k - 1],
                two_sem.at[1, group, k - 1],
                tm_peers[k - 1],
            )
            for k in range(1, n_tm)
        ]

    hid_rows = sum(frames + 2 * reach(l) for l in range(LAYERS))

    def head(s):
        for owner in range(n_tm):
            gs_copies[s * n_tm + owner].wait_recv()
            at = owner * cols + s * sub
            total = dot_tn(hid_mine[hid_rows : hid_rows + frames, :], gs[:, at : at + sub])
            total = total + dot_tn(hid_far[hid_rows : hid_rows + frames, :], gs_far[:, at : at + sub])
            send_h[s, owner] = total.astype(BF16)

            @pl.when(t == owner)
            def _():
                acc_h[s] = total

        send_two(LAYERS + s, send_h.at[s], recv_h.at[s])

    def conv(layer):
        gp_copies[layer].wait_recv()
        d = reach(layer)
        base = sum(frames + 2 * reach(l) for l in range(layer))
        for k in range(3):
            at = base + k * d
            total = dot_tn(hid_mine[at : at + frames, :], gpads[layer][d : d + frames, :])
            total = total + dot_tn(hid_far[at : at + frames, :], gp_far[layer])
            for owner in range(n_tm):
                chunk = total[:, owner * conv_cols : (owner + 1) * conv_cols]
                send_c[layer, owner, k] = chunk.astype(BF16)

                @pl.when(t == owner)
                def _():
                    acc_c[layer, k] = chunk

        send_two(layer, send_c.at[layer], recv_c.at[layer])

    def finish_two(group):
        for copy in two[group]:
            copy.wait_recv()
        if group < LAYERS:
            for k in range(3):
                total = acc_c[group, k]
                for slot in range(n_tm - 1):
                    total = total + recv_c[group, slot, k].astype(F32)
                acc_c[group, k] = total
                done_c[group, k] = total.astype(BF16)
        else:
            total = acc_h[group - LAYERS]
            for slot in range(n_tm - 1):
                total = total + recv_h[group - LAYERS, slot].astype(F32)
            acc_h[group - LAYERS] = total
            done_h[group - LAYERS] = total.astype(BF16)
        three[group] = []
        for k in range(1, n_q):
            part = pl.ds(pl.multiple_of(q_next[k - 1] * rows, rows), rows)
            if group < LAYERS:
                src, dst = done_c.at[group, :, part], last_c.at[group, k - 1]
            else:
                src, dst = done_h.at[group - LAYERS, part], last_h.at[group - LAYERS, k - 1]
            three[group].append(
                start(
                    src,
                    dst,
                    three_sem.at[0, group, k - 1],
                    three_sem.at[1, group, k - 1],
                    q_peers[k - 1],
                )
            )

    def finish_three(group):
        for copy in three[group]:
            copy.wait_recv()
        part = pl.ds(pl.multiple_of(q * rows, rows), rows)
        if group < LAYERS:
            for k in range(3):
                total = acc_c[group, k, part, :]
                for slot in range(n_q - 1):
                    total = total + last_c[group, slot, k].astype(F32)
                out_conv[group, k] = total
        else:
            s = group - LAYERS
            total = acc_h[s, part, :]
            for slot in range(n_q - 1):
                total = total + last_h[s, slot].astype(F32)
            out_head[:, s * sub : (s + 1) * sub] = total

    for load in gs_loads:
        load.wait()
    hid_load.wait()
    hid_copy.wait_recv()
    head(0)
    head(1)
    head_back()
    make_gpre(3)
    head(2)
    cw_load.wait()
    back(3)
    make_gpre(2)
    conv(3)
    back(2)
    make_gpre(1)
    conv(2)
    finish_two(4)
    back(1)
    make_gpre(0)
    conv(1)
    finish_two(5)
    conv(0)
    head(3)
    head(4)
    finish_two(6)
    finish_three(4)
    finish_two(3)
    finish_three(5)
    finish_two(2)
    finish_three(6)
    finish_two(1)
    finish_three(3)
    finish_two(0)
    finish_three(2)
    finish_two(7)
    finish_three(1)
    finish_two(8)
    for group in (0, 7, 8):
        finish_three(group)
    for copy in sent:
        copy.wait_send()


def backward(hid_mine, hid_other, gs, hw, cw, pres, mask):
    n_read, n_tm = lax.axis_size("read"), lax.axis_size("tm")
    frames, scores = gs.shape
    width = cw.shape[-1]
    n_q, half, rows = n_read // 2, width // 2, width // n_read
    cols, conv_cols = scores // n_tm, width // n_tm
    sub = cols // HEAD_GROUPS
    groups = LAYERS + HEAD_GROUPS
    vmem = pl.BlockSpec(memory_space=pltpu.VMEM)
    dma = pltpu.SemaphoreType.DMA
    return pl.pallas_call(
        functools.partial(backward_kernel, n_read, n_tm),
        out_shape=(
            jax.ShapeDtypeStruct((LAYERS, 3, rows, conv_cols), F32),
            jax.ShapeDtypeStruct((rows, cols), F32),
        ),
        in_specs=[pl.BlockSpec(memory_space=pl.ANY)] * 9 + [vmem],
        out_specs=(vmem, vmem),
        scratch_shapes=[
            pltpu.VMEM(hid_mine.shape, BF16),
            pltpu.VMEM(gs.shape, BF16),
            pltpu.VMEM(hw.shape, BF16),
            pltpu.VMEM((LAYERS - 1,) + cw.shape[1:], BF16),
        ]
        + [pltpu.VMEM((frames, width), F32)] * LAYERS
        + [
            pltpu.VMEM(hid_mine.shape, BF16),
            pltpu.VMEM((frames, scores), BF16),
            pltpu.VMEM((frames, width), F32),
        ]
        + [pltpu.VMEM((frames + 2 * reach(l), width), BF16) for l in range(LAYERS)]
        + [
            pltpu.VMEM((LAYERS, frames, width), BF16),
            pltpu.VMEM((HEAD_GROUPS, n_tm, half, sub), BF16),
            pltpu.VMEM((HEAD_GROUPS, n_tm - 1, half, sub), BF16),
            pltpu.VMEM((HEAD_GROUPS, half, sub), F32),
            pltpu.VMEM((HEAD_GROUPS, half, sub), BF16),
            pltpu.VMEM((HEAD_GROUPS, n_q - 1, rows, sub), BF16),
            pltpu.VMEM((LAYERS, n_tm, 3, half, conv_cols), BF16),
            pltpu.VMEM((LAYERS, n_tm - 1, 3, half, conv_cols), BF16),
            pltpu.VMEM((LAYERS, 3, half, conv_cols), F32),
            pltpu.VMEM((LAYERS, 3, half, conv_cols), BF16),
            pltpu.VMEM((LAYERS, n_q - 1, 3, rows, conv_cols), BF16),
            dma((2,)),
            dma((2, HEAD_GROUPS, n_tm)),
            dma((2, LAYERS)),
            dma((2, 2, LAYERS)),
            dma((2, groups, n_tm - 1)),
            dma((2, groups, n_q - 1)),
            dma((HEAD_GROUPS,)),
            dma((HEAD_GROUPS,)),
            dma((LAYERS + 2,)),
        ],
        compiler_params=pltpu.CompilerParams(
            collective_id=1, has_side_effects=True, vmem_limit_bytes=60 * 2**20
        ),
    )(hid_mine, hid_other, gs, hw, cw, *pres, mask)


def forward_kernel(
    n_read,
    n_tm,
    x,
    cw_hbm,
    mask,
    out_mine,
    out_other,
    out_hidden,
    pre0,
    pre1,
    pre2,
    pre3,
    hp0,
    hp1,
    hp2,
    hp3,
    cw,
    cw_sem,
    halo_sem,
):
    pres, pads = (pre0, pre1, pre2, pre3), (hp0, hp1, hp2, hp3)
    frames, width = x.shape
    half, rows = width // 2, width // n_read
    r, t = lax.axis_index("read"), lax.axis_index("tm")
    core = lax.rem(r, 2)
    loads = [
        pltpu.make_async_copy(cw_hbm.at[l], cw.at[l], cw_sem.at[l]) for l in range(LAYERS)
    ]
    for load in loads:
        load.start()
    hp0[reach(0) : reach(0) + frames, :] = x[...]

    barrier = pltpu.get_barrier_semaphore()
    for k in range(1, n_tm):
        pl.semaphore_signal(
            barrier, inc=1, device_id={"tm": lax.rem(t + k, n_tm)}, device_id_type=MESH
        )
    pl.semaphore_wait(barrier, n_tm - 1)

    channel = lax.broadcasted_iota(jnp.int32, (width, half), 0)
    place = lax.broadcasted_iota(jnp.int32, (width, half), 1)
    wanted = 2 * rows * (place // rows) + lax.rem(place, rows)
    pick_mine = (channel == wanted + rows * core).astype(F32).astype(BF16)
    pick_other = (channel == wanted + rows * (1 - core)).astype(F32).astype(BF16)

    def deal(value, at):
        size = value.shape[0]
        for out, pick in ((out_mine, pick_mine), (out_other, pick_other)):
            out[at : at + size, :] = jnp.dot(
                value, pick, preferred_element_type=F32
            ).astype(BF16)

    base = 0
    for layer in range(LAYERS):
        d = reach(layer)
        pad = pads[layer]

        def halo(side, first, landing, to, pad=pad, d=d, layer=layer):
            return pltpu.make_async_remote_copy(
                src_ref=pad.at[pl.ds(first, d)],
                dst_ref=pad.at[pl.ds(landing, d)],
                send_sem=halo_sem.at[side, 0, layer],
                recv_sem=halo_sem.at[side, 1, layer],
                device_id={"tm": lax.rem(t + to, n_tm)},
                device_id_type=MESH,
            )

        before = halo(0, d, d + frames, n_tm - 1)
        after = halo(1, frames, 0, 1)

        @pl.when(t > 0)
        def _():
            before.start()

        @pl.when(t < n_tm - 1)
        def _():
            after.start()

        @pl.when(t == 0)
        def _():
            pad[0:d, :] = jnp.zeros((d, width), BF16)

        @pl.when(t == n_tm - 1)
        def _():
            pad[d + frames : d + frames + d, :] = jnp.zeros((d, width), BF16)

        loads[layer].wait()
        pre = pres[layer]
        pre[...] = jnp.dot(pad[d : d + frames, :], cw[layer, 1], preferred_element_type=F32)
        deal(pad[d : d + frames, :], base + d)

        @pl.when(t < n_tm - 1)
        def _():
            before.wait_recv()

        @pl.when(t > 0)
        def _():
            after.wait_recv()

        pre[...] += jnp.dot(pad[0:frames, :], cw[layer, 0], preferred_element_type=F32)
        pre[...] += jnp.dot(
            pad[2 * d : 2 * d + frames, :], cw[layer, 2], preferred_element_type=F32
        )
        total = pre[...]
        hidden = (
            mask[...]
            * (pad[d : d + frames, :].astype(F32) + total * (1.0 / (1.0 + jnp.exp(-total))))
        ).astype(BF16)
        if layer < LAYERS - 1:
            pads[layer + 1][2 * d : 2 * d + frames, :] = hidden
        else:
            out_hidden[...] = hidden
        deal(pad[0:d, :], base)
        deal(pad[d + frames : d + frames + d, :], base + d + frames)

        @pl.when(t > 0)
        def _():
            before.wait_send()

        @pl.when(t < n_tm - 1)
        def _():
            after.wait_send()

        base += frames + 2 * d
    deal(out_hidden[...], base)


def forward(x, cw, mask):
    n_read, n_tm = lax.axis_size("read"), lax.axis_size("tm")
    frames, width = x.shape
    total = frames + sum(frames + 2 * reach(l) for l in range(LAYERS))
    vmem = pl.BlockSpec(memory_space=pltpu.VMEM)
    dma = pltpu.SemaphoreType.DMA
    return pl.pallas_call(
        functools.partial(forward_kernel, n_read, n_tm),
        out_shape=[
            jax.ShapeDtypeStruct((total, width // 2), BF16),
            jax.ShapeDtypeStruct((total, width // 2), BF16),
            jax.ShapeDtypeStruct((frames, width), BF16),
        ]
        + [jax.ShapeDtypeStruct((frames, width), F32)] * LAYERS,
        in_specs=[vmem, pl.BlockSpec(memory_space=pl.ANY), vmem],
        out_specs=[vmem] * (3 + LAYERS),
        scratch_shapes=[
            pltpu.VMEM((frames + 2 * reach(l), width), BF16) for l in range(LAYERS)
        ]
        + [pltpu.VMEM(cw.shape, BF16), dma((LAYERS,)), dma((2, 2, LAYERS))],
        compiler_params=pltpu.CompilerParams(
            collective_id=0, has_side_effects=True, vmem_limit_bytes=48 * 2**20
        ),
    )(x, cw, mask)


def on_device(student_in, teacher_rows, valid, conv_weight, head_weight, teacher_head_weight):
    reads_dev, frames, width = student_in.shape
    n_read = lax.axis_size("read")
    scores = head_weight.shape[1]
    loss_scale = scores / (
        3.0 * math.sqrt(reads_dev * n_read * frames * lax.axis_size("tm"))
    )
    first_frame = lax.axis_index("tm") * frames
    positions = first_frame + jnp.arange(frames, dtype=jnp.int32)
    mask = (positions < valid[0]).astype(F32)[:, None]
    mine, other, hidden, *pres = forward(student_in[0], conv_weight, mask)
    squash = jnp.tanh(jnp.dot(hidden, head_weight, preferred_element_type=F32))
    teacher = 5.0 * jnp.tanh(
        jnp.dot(teacher_rows[0], teacher_head_weight, preferred_element_type=F32)
    )
    exp_teacher, exp_student = jnp.exp(teacher), jnp.exp(5.0 * squash)
    prob_teacher = exp_teacher * (1.0 / jnp.sum(exp_teacher, axis=-1, keepdims=True))
    prob_student = exp_student * (1.0 / jnp.sum(exp_student, axis=-1, keepdims=True))
    g_score = (
        loss_scale * mask * (prob_student - prob_teacher) * 5.0 * (1.0 - squash * squash)
    ).astype(BF16)
    return backward(mine, other, g_score, head_weight, conv_weight, pres, mask)


def solution(mesh):
    return jax.shard_map(
        on_device,
        mesh=mesh,
        in_specs=(P("read", "tm", None), P("read", "tm", None), P("read"), P(), P(), P()),
        out_specs=(P(None, None, "read", "tm"), P("read", "tm")),
        check_vma=False,
    )
```
